256 devices in a mesh: dp: 8 (over x, z_lo), tensor: 32 (over y, z_hi, core).
Axes of the slice: x: 4, y: 4, z: 8 (z_hi: 4, z_lo: 2; z = z_hi * 2 + z_lo), core: 2. Of those that a mesh axis runs over, the one named last changes fastest.
Arguments:
- hidden_in: bfloat16 [1024, 12288], P('dp', 'tensor'), may hold values from -300 to 300, as said below
- ln_gain: float32 [12288], P('tensor'), may hold values from 0.5 to 1.5
- ln_bias: float32 [12288], P('tensor'), may hold values from -3 to 3
- q_weight: bfloat16 [12288, 12288], P('dp', 'tensor'), may hold values from -2 to 2
- grad_query: bfloat16 [1024, 12288], P('dp', 'tensor'), may hold values from -6 to 6
Outputs:
- grad_input: float32 [1024, 12288], P('dp', 'tensor')
- grad_weight: float32 [12288, 12288], P('dp', 'tensor')
- grad_gain: float32 [12288], P('tensor')
- grad_bias: float32 [12288], P('tensor')
The draws below stay inside these ranges and needn't reach their ends.
Inputs may be any that keep to these rules, and one draw needn't show every extreme that they name: `hidden_in`: finite values.
All inputs are finite; a program needn't handle non-finite values.
Results may differ from the reference program's by a relative error of at most 0.0029.
Values may be sent and summed in bfloat16 or wider, within the bound.
No kernel may reach another device: no remote copies, remote signals or barrier semaphores. Data moves between devices by JAX's collectives and lax.ppermute only.
A program may use at most 128 MiB of HBM per device.

```python
import jax
import jax.numpy as jnp
from jax import lax

D = 12288
TOKENS = 1024


def feature_profile(key):
    key = jax.random.fold_in(key, 5)
    ramp = jnp.exp(jnp.arange(D, dtype=jnp.float32) / D * jnp.log(4.0))
    rough = jnp.exp(jax.random.uniform(key, (D,), jnp.float32, -0.7, 0.7))
    return ramp * rough


def draw_hidden_in(key, part):
    profile = feature_profile(key)
    key = jax.random.fold_in(key, 11)
    keys = jax.random.split(key, 6)
    row_scale = jnp.exp(jax.random.uniform(keys[0], (TOKENS, 1), jnp.float32) * jnp.log(10.0))
    column_pos = jnp.arange(D, dtype=jnp.float32)[None, :] / D
    col_scale = jnp.exp(column_pos * jnp.log(3.0)) * jnp.exp(jax.random.uniform(keys[1], (1, D), jnp.float32, -0.35, 0.35))
    offset = jax.random.normal(keys[2], (TOKENS, 1), jnp.float32) * 2.0
    loading = jax.random.normal(keys[5], (TOKENS, 1), jnp.float32)
    base = jax.random.normal(keys[3], (TOKENS, D), jnp.float32)
    values = (base * col_scale + loading * profile[None, :] + offset) * row_scale
    return jnp.clip(values, -300.0, 300.0).astype(jnp.bfloat16)


def draw_q_weight(key, part):
    profile = feature_profile(key)
    key = jax.random.fold_in(key, 23)
    keys = jax.random.split(key, 2)
    noise = jax.random.normal(keys[0], (D, D), jnp.float32) * D ** (-0.5)
    column_load = jax.random.normal(keys[1], (1, D), jnp.float32) * (0.5 * D ** (-0.5))
    values = noise + profile[:, None] * column_load
    return jnp.clip(values, -2.0, 2.0).astype(jnp.bfloat16)


def levels(own_key, extent, cuts, low, top_value):
    level, own = 1.0, jax.random.fold_in(own_key, 6)
    for axis_at, shards_of in cuts:
        steps = jnp.exp(jax.random.uniform(jax.random.fold_in(own, axis_at), (shards_of,), jnp.float32, low / len(cuts), top_value / len(cuts)))
        level = level * jnp.repeat(steps, extent[axis_at] // shards_of).reshape([-1 if axis == axis_at else 1 for axis in range(len(extent))])
    return level


def centred(rng, dims, deviation, bound, cuts=(), kind=jnp.bfloat16):
    array = deviation * jax.random.normal(rng, dims, jnp.float32)
    if cuts:
        array = array * levels(rng, dims, cuts, -0.22, 0.18)
    return jnp.clip(array, -bound, bound).astype(kind)


def setup_inputs(seed: int = 0) -> dict:
    streams_of = jax.random.split(jax.random.key(seed), 6)
    hidden_in = draw_hidden_in(jax.random.fold_in(streams_of[5], 71), 0)
    ln_gain = jnp.clip(1.0 + 0.1 * jax.random.normal(streams_of[1], (D,), jnp.float32), 0.5, 1.5)
    ln_bias = centred(streams_of[2], (D,), 0.5, 3.0, ((0, 32),), jnp.float32)
    q_weight = draw_q_weight(jax.random.fold_in(streams_of[5], 71), 0)
    grad_query = centred(streams_of[4], (TOKENS, D), 1.0, 6.0, ((0, 8), (1, 32)))
    return {"hidden_in": hidden_in, "ln_gain": ln_gain, "ln_bias": ln_bias, "q_weight": q_weight, "grad_query": grad_query}


def reference(hidden_in, ln_gain, ln_bias, q_weight, grad_query):
    values = hidden_in.astype(jnp.float32)
    row_sum = lax.optimization_barrier(jnp.sum(values, axis=1))
    row_square = lax.optimization_barrier(jnp.sum(values * values, axis=1))
    row_mean = row_sum / D
    row_var = row_square / D - row_mean * row_mean
    inv_std = lax.rsqrt(row_var + 1e-05)
    standard = (values - row_mean[:, None]) * inv_std[:, None]
    normed = (standard * ln_gain + ln_bias).astype(jnp.bfloat16)
    grad_weight = lax.dot_general(normed, grad_query, (((0,), (0,)), ((), ())), preferred_element_type=jnp.float32)
    grad_normed = lax.dot_general(grad_query, q_weight, (((1,), (1,)), ((), ())), preferred_element_type=jnp.float32)
    grad_gain = lax.optimization_barrier(jnp.sum(grad_normed * standard, axis=0))
    grad_bias = lax.optimization_barrier(jnp.sum(grad_normed, axis=0))
    scaled = grad_normed * ln_gain
    first = lax.optimization_barrier(jnp.sum(scaled, axis=1)) / D
    second = lax.optimization_barrier(jnp.sum(scaled * standard, axis=1)) / D
    grad_input = inv_std[:, None] * (scaled - first[:, None] - standard * second[:, None])
    return (grad_input, grad_weight, grad_gain, grad_bias)
```

```python
import jax
import jax.numpy as jnp
from jax import lax
from jax.sharding import PartitionSpec as P

AXES = ("dp", "tensor")
DATA, TENSOR = 8, 32
CAP = 32768.0


def flat(x, zl, y, zh, c):
    return ((x * 2 + zl) * 4 + y) * 8 + zh * 2 + c


def table(move):
    pairs = []
    for d in range(DATA):
        for t in range(TENSOR):
            place = (d // 2, d % 2, t // 8, (t // 2) % 4, t % 2)
            pairs.append((flat(*place), flat(*move(*place))))
    return pairs


def to_owner(k):
    def move(x, zl, y, zh, c):
        s = (zh + k) % 4
        return (y, s % 2, x, 2 * zl + s // 2, c)

    return table(move)


CORE = table(lambda x, zl, y, zh, c: (x, zl, y, zh, 1 - c))
ALONG_Y = [table(lambda x, zl, y, zh, c, k=k: (x, zl, (y + k) % 4, zh, c)) for k in range(4)]
OWNER = [to_owner(k) for k in range(4)]
HOLDER = [[(b, a) for a, b in pairs] for pairs in OWNER]


def send(array, pairs):
    return lax.ppermute(array, AXES, pairs)


def after(array, *others):
    return lax.optimization_barrier((array,) + others)[0]


def total(array, axis, size):
    copies = jnp.broadcast_to(array[None], (size,) + array.shape)
    copies = lax.all_to_all(copies, axis, split_axis=0, concat_axis=0, tiled=True)
    return jnp.sum(copies, axis=0)


def pack(values, power):
    body = (values * jnp.exp2(power)).astype(jnp.float16)
    tail = jnp.full((16, values.shape[1]), power, jnp.float32).astype(jnp.float16)
    return jnp.concatenate([body, tail], axis=0)


def unpack(message):
    power = message[-16, 0].astype(jnp.float32)
    return message[:-16].astype(jnp.float32) * jnp.exp2(-power), power


def power_for(bound):
    return jnp.clip(jnp.floor(jnp.log2(CAP / bound)), -100.0, 100.0)


def body(hidden_in, ln_gain, ln_bias, q_weight, grad_query):
    tokens, width = hidden_in.shape
    d, t = lax.axis_index("dp"), lax.axis_index("tensor")
    y, zh, c = t // 8, (t // 2) % 4, t % 2
    features = width * TENSOR

    quarters = q_weight.reshape(2, 2, width, width)
    mine = lax.dynamic_index_in_dim(quarters, c, axis=1, keepdims=False).reshape(2 * width, width)
    theirs = lax.dynamic_index_in_dim(quarters, 1 - c, axis=1, keepdims=False).reshape(2 * width, width)
    theirs = send(theirs, CORE)

    query = jnp.broadcast_to(grad_query[None], (DATA,) + grad_query.shape)
    query = lax.all_to_all(query, "dp", split_axis=0, concat_axis=0, tiled=True).reshape(4, 2 * tokens, width)
    query_other = send(query, CORE)

    highest = lambda a: jnp.max(jnp.abs(a)).astype(jnp.float32)
    bound = width * (highest(query) * highest(mine) + highest(query_other) * highest(theirs))
    power = power_for(bound)

    at = [(y + k) % 4 for k in range(4)]
    own_tokens = [lax.dynamic_index_in_dim(query, at[k], axis=0, keepdims=False) for k in range(4)]
    other_tokens = [lax.dynamic_index_in_dim(query_other, at[k], axis=0, keepdims=False) for k in range(4)]
    rows_by_rows = (((1,), (1,)), ((), ()))

    def part(k):
        return lax.dot_general(
            own_tokens[k], mine, rows_by_rows, preferred_element_type=jnp.float32
        ) + lax.dot_general(other_tokens[k], theirs, rows_by_rows, preferred_element_type=jnp.float32)

    sent = [pack(part(k), power) for k in (2, 1, 3)]
    parts = [unpack(send(m, ALONG_Y[k])) for m, k in zip(sent, (2, 1, 3))]

    values = hidden_in.astype(jnp.float32)
    sums = jnp.stack([jnp.sum(values, axis=1), jnp.sum(values * values, axis=1)])
    row_sum, row_square = total(after(sums, *sent), "tensor", TENSOR)
    row_mean = row_sum / features
    row_var = row_square / features - row_mean * row_mean
    inv_std = lax.rsqrt(row_var + 1e-05)
    standard = (values - row_mean[:, None]) * inv_std[:, None]
    normed = (standard * ln_gain + ln_bias).astype(jnp.bfloat16)

    summed = part(0) + parts[0][0] + parts[1][0] + parts[2][0]
    bound = bound + CAP * (jnp.exp2(-parts[0][1]) + jnp.exp2(-parts[1][1]) + jnp.exp2(-parts[2][1]))
    power = power_for(bound)
    summed = summed.reshape(2, tokens, 2, width)

    grad_normed = None
    for k in range(4):
        s = (zh + k) % 4
        tile = lax.dynamic_slice(summed, (s % 2, 0, s // 2, 0), (1, tokens, 1, width)).reshape(tokens, width)
        piece = unpack(send(pack(tile, power), OWNER[k]))[0]
        grad_normed = piece if grad_normed is None else grad_normed + piece

    tiles = [send(normed, HOLDER[k]) for k in range(4)]
    tiles = lax.dynamic_slice_in_dim(jnp.stack(tiles + tiles[:3]), (4 - zh) % 4, 4, axis=0)
    block = tiles.reshape(2, 2, tokens, width).transpose(1, 2, 0, 3).reshape(2 * tokens, 2 * width)
    blocks = [block] + [send(block, ALONG_Y[k]) for k in (1, 2, 3)]

    def weight_part(columns):
        out = 0.0
        for k in range(4):
            out = out + lax.dot_general(
                blocks[k], columns[(4 - k) % 4], (((0,), (0,)), ((), ())), preferred_element_type=jnp.float32
            )
        return out

    received = send(weight_part(other_tokens), CORE).reshape(2, width, width)
    kept = weight_part(own_tokens).reshape(2, width, width)
    grad_weight = jnp.where(
        c == 0, jnp.stack([kept, received], axis=1), jnp.stack([received, kept], axis=1)
    ).reshape(4 * width, width)

    scaled = grad_normed * ln_gain
    first, second = total(
        jnp.stack([jnp.sum(scaled, axis=1), jnp.sum(scaled * standard, axis=1)]), "tensor", TENSOR
    )
    first, second = first / features, second / features
    grad_input = inv_std[:, None] * (scaled - first[:, None] - standard * second[:, None])
    grad_gain, grad_bias = total(
        jnp.stack([jnp.sum(grad_normed * standard, axis=0), jnp.sum(grad_normed, axis=0)]), "dp", DATA
    )
    return (grad_input, grad_weight, grad_gain, grad_bias)


def solution(mesh):
    placed = (P("dp", "tensor"), P("tensor"), P("tensor"), P("dp", "tensor"), P("dp", "tensor"))
    return jax.shard_map(
        body,
        mesh=mesh,
        in_specs=placed,
        out_specs=(P("dp", "tensor"), P("dp", "tensor"), P("tensor"), P("tensor")),
        check_vma=False,
    )
```

```python
import jax
import jax.numpy as jnp
from jax import lax
from jax.experimental import pallas as pl
from jax.experimental.pallas import tpu as pltpu
from jax.sharding import PartitionSpec as P

AXES = ("dp", "tensor")
DATA, TENSOR = 8, 32
CAP = 32768.0
ROWS_BY_ROWS = (((1,), (1,)), ((), ()))
COLUMNS_BY_COLUMNS = (((0,), (0,)), ((), ()))


def flat(x, zl, y, zh, c):
    return ((x * 2 + zl) * 4 + y) * 8 + zh * 2 + c


def table(move):
    pairs = []
    for d in range(DATA):
        for t in range(TENSOR):
            place = (d // 2, d % 2, t // 8, (t // 2) % 4, t % 2)
            pairs.append((flat(*place), flat(*move(*place))))
    return pairs


def to_owner(k):
    def move(x, zl, y, zh, c):
        s = (zh + k) % 4
        return (y, s % 2, x, 2 * zl + s // 2, c)

    return table(move)


CORE = table(lambda x, zl, y, zh, c: (x, zl, y, zh, 1 - c))
ALONG_X = [
    [table(lambda x, zl, y, zh, c, i=i, j=j: ((x + i) % 4, zl ^ j, y, zh, c)) for j in range(2)] for i in range(4)
]
ALONG_Y = [table(lambda x, zl, y, zh, c, k=k: (x, zl, (y + k) % 4, zh, c)) for k in range(4)]
OWNER = [to_owner(k) for k in range(4)]
HOLDER = table(lambda x, zl, y, zh, c: (y, zh // 2, x, 2 * (zh % 2) + zl, c))
Z_GROUPS = [[8 * y + 2 * z + c for z in range(4)] for y in range(4) for c in range(2)]


def send(array, pairs):
    return lax.ppermute(array, AXES, pairs)


def after(array, *others):
    return lax.optimization_barrier((array,) + others)[0]


def exchange(array, axis, groups=None):
    return lax.all_to_all(array, axis, split_axis=0, concat_axis=0, tiled=True, axis_index_groups=groups)


def copies(array, size):
    return jnp.broadcast_to(array[None], (size,) + array.shape)


def highest(array):
    return jnp.max(jnp.abs(array), keepdims=True).reshape(1, 1).astype(jnp.float32)


def weight_kernel(at_ref, first_ref, second_ref, third_ref, fourth_ref, columns_ref, out_ref):
    total = None
    for k, block_ref in enumerate((first_ref, second_ref, third_ref, fourth_ref)):
        term = lax.dot_general(
            block_ref[0], columns_ref[at_ref[k]], COLUMNS_BY_COLUMNS, preferred_element_type=jnp.float32
        )
        total = term if total is None else total + term
    out_ref[...] = total.reshape(out_ref.shape)


def fill_kernel(core_ref, values_ref, whole_ref, out_ref):
    out_ref[...] = values_ref[...].reshape(out_ref.shape)


def weight_part(at, blocks, columns, place=None):
    halves, rows, width = blocks[0].shape
    block = pl.BlockSpec((1, rows, width), lambda i, at: (i, 0, 0))
    if place is None:
        out_shape = jax.ShapeDtypeStruct((halves, width, width), jnp.float32)
        out_spec = pl.BlockSpec((1, width, width), lambda i, at: (i, 0, 0))
    else:
        out_shape = jax.ShapeDtypeStruct((halves, 2, width, width), jnp.float32)
        out_spec = pl.BlockSpec((1, 1, width, width), lambda i, at: (i, at[4], 0, 0))
    return pl.pallas_call(
        weight_kernel,
        out_shape=out_shape,
        grid_spec=pltpu.PrefetchScalarGridSpec(
            num_scalar_prefetch=1,
            grid=(halves,),
            in_specs=[block] * 4 + [pl.BlockSpec(columns.shape, lambda i, at: (0, 0, 0))],
            out_specs=out_spec,
        ),
        compiler_params=pltpu.CompilerParams(vmem_limit_bytes=32 * 1024 * 1024),
        cost_estimate=pl.CostEstimate(
            flops=8 * halves * rows * width * width, bytes_accessed=8 * halves * rows * width, transcendentals=0
        ),
    )(at, *blocks, columns)


def fill(core, values, whole):
    halves, width, _ = values.shape
    return pl.pallas_call(
        fill_kernel,
        out_shape=jax.ShapeDtypeStruct(whole.shape, whole.dtype),
        grid_spec=pltpu.PrefetchScalarGridSpec(
            num_scalar_prefetch=1,
            grid=(halves,),
            in_specs=[
                pl.BlockSpec((1, width, width), lambda i, core: (i, 0, 0)),
                pl.BlockSpec(memory_space=pl.ANY),
            ],
            out_specs=pl.BlockSpec((1, 1, width, width), lambda i, core: (i, core[0], 0, 0)),
        ),
        input_output_aliases={2: 0},
        compiler_params=pltpu.CompilerParams(vmem_limit_bytes=32 * 1024 * 1024),
    )(core, values, whole)


def body(hidden_in, ln_gain, ln_bias, q_weight, grad_query):
    tokens, width = hidden_in.shape
    d, t = lax.axis_index("dp"), lax.axis_index("tensor")
    x, zl, y, zh, c = d // 2, d % 2, t // 8, (t // 2) % 4, t % 2
    features = width * TENSOR

    there = send(grad_query, ALONG_X[0][1])
    pair = jnp.where(zl == 0, jnp.concatenate([grad_query, there]), jnp.concatenate([there, grad_query]))
    query = jnp.stack([pair] + [send(pair, ALONG_X[i][0]) for i in (1, 2, 3)])

    values = hidden_in.astype(jnp.float32)
    told = jnp.concatenate([jnp.sum(values, axis=1), jnp.sum(values * values, axis=1)])
    told = exchange(copies(after(told, there), TENSOR), "tensor")
    query, told = lax.optimization_barrier((query, told))
    sums = jnp.sum(told, axis=0) / features
    row_mean = sums[:tokens, None]
    inv_std = lax.rsqrt(sums[tokens:, None] - row_mean * row_mean + 1e-05)
    standard = (values - row_mean) * inv_std
    normed = (standard * ln_gain + ln_bias).astype(jnp.bfloat16)

    quarters = q_weight.reshape(2, 2, width, width)
    mine = lax.dynamic_index_in_dim(quarters, c, axis=1, keepdims=False).reshape(2 * width, width)
    theirs = lax.dynamic_index_in_dim(quarters, 1 - c, axis=1, keepdims=False).reshape(2 * width, width)
    theirs = send(theirs, CORE)
    query_other = send(query, CORE)
    bound = width * highest(query) * highest(q_weight)
    bound = bound + send(bound, CORE)
    power = jnp.clip(jnp.floor(jnp.log2(CAP / bound)), -100.0, 100.0)

    at = [(x - y - k) % 4 for k in range(4)]
    own_tokens = [lax.dynamic_index_in_dim(query, at[k], axis=0, keepdims=False) for k in range(4)]
    other_tokens = [lax.dynamic_index_in_dim(query_other, at[k], axis=0, keepdims=False) for k in range(4)]

    extended = 2 * tokens + 16
    last = lax.broadcasted_iota(jnp.int32, (extended, 2 * width), 0) >= 2 * tokens
    longer = lambda array: jnp.pad(array, ((0, 16), (0, 0)))
    sent, received = [], []
    for k in (2, 1, 3, 0):
        part = lax.dot_general(
            longer(own_tokens[k]), mine, ROWS_BY_ROWS, preferred_element_type=jnp.float32
        ) + lax.dot_general(longer(other_tokens[k]), theirs, ROWS_BY_ROWS, preferred_element_type=jnp.float32)
        sent.append(jnp.where(last, power, part * jnp.exp2(power)).astype(jnp.float16))
        received.append(send(sent[-1], ALONG_Y[k]) if k else sent[-1])


    normed = send(after(normed, *sent), HOLDER)
    *received, normed = lax.optimization_barrier((*received, normed))

    powers = [lax.dynamic_slice(message, (2 * tokens, 0), (1, 1)).astype(jnp.float32) for message in received]
    power = jnp.minimum(jnp.minimum(powers[0], powers[1]), jnp.minimum(powers[2], powers[3])) - 2.0
    scales = [jnp.exp2(power - other) for other in powers]
    last = lax.broadcasted_iota(jnp.int32, (tokens + 16, width), 0) >= tokens
    pieces = []
    for k in range(4):
        s = (zh + k) % 4
        cut = ((s % 2) * tokens, (s // 2) * width)
        piece = sum(
            lax.dynamic_slice(message, cut, (tokens + 16, width)).astype(jnp.float32) * scale
            for message, scale in zip(received, scales)
        )
        pieces.append(jnp.where(last, power, piece).astype(jnp.float16))
    pieces = [send(piece, OWNER[k]) for k, piece in enumerate(pieces)]

    block = exchange(copies(normed, 4), "tensor", Z_GROUPS).reshape(2, 2 * tokens, width)
    pieces, block = lax.optimization_barrier((pieces, block))
    blocks = [block] + [send(block, ALONG_Y[k]) for k in (1, 2, 3)]

    grad_normed = sum(
        piece[:tokens].astype(jnp.float32) * jnp.exp2(-piece[tokens : tokens + 1].astype(jnp.float32)) for piece in pieces
    )

    scaled = grad_normed * ln_gain
    told = jnp.concatenate([jnp.sum(scaled, axis=1), jnp.sum(scaled * standard, axis=1)])
    told = exchange(copies(told, TENSOR), "tensor")
    sums = jnp.stack([jnp.sum(grad_normed * standard, axis=0), jnp.sum(grad_normed, axis=0)])
    other = send(sums, ALONG_X[0][1])
    told, other, blocks = lax.optimization_barrier((told, other, blocks))
    sums = sums + other
    sums = sums + send(sums, ALONG_X[1][0]) + send(sums, ALONG_X[2][0]) + send(sums, ALONG_X[3][0])
    told = jnp.sum(told, axis=0) / features
    grad_input = inv_std * (scaled - told[:tokens, None] - standard * told[tokens:, None])

    at = jnp.stack([(x - y + k) % 4 for k in range(4)] + [c]).astype(jnp.int32)
    grad_other = send(weight_part(at, blocks, query_other), CORE)
    grad_mine = weight_part(at, blocks, query, c)
    grad_weight = fill((1 - c).astype(jnp.int32).reshape(1), grad_other, grad_mine).reshape(4 * width, width)
    return (grad_input, grad_weight, sums[0], sums[1])


def solution(mesh):
    placed = (P("dp", "tensor"), P("tensor"), P("tensor"), P("dp", "tensor"), P("dp", "tensor"))
    return jax.shard_map(
        body,
        mesh=mesh,
        in_specs=placed,
        out_specs=(P("dp", "tensor"), P("dp", "tensor"), P("tensor"), P("tensor")),
        check_vma=False,
    )
```

```python
import jax
import jax.numpy as jnp
from jax import lax
from jax.experimental import pallas as pl
from jax.experimental.pallas import tpu as pltpu
from jax.sharding import PartitionSpec as P

AXES = ("dp", "tensor")
DATA, TENSOR = 8, 32
CAP = 32768.0
ROWS_BY_ROWS = (((1,), (1,)), ((), ()))
COLUMNS_BY_COLUMNS = (((0,), (0,)), ((), ()))


def flat(x, zl, y, zh, c):
    return ((x * 2 + zl) * 4 + y) * 8 + zh * 2 + c


def table(move):
    pairs = []
    for d in range(DATA):
        for t in range(TENSOR):
            place = (d // 2, d % 2, t // 8, (t // 2) % 4, t % 2)
            pairs.append((flat(*place), flat(*move(*place))))
    return pairs


def to_owner(k):
    def move(x, zl, y, zh, c):
        s = (zh + k) % 4
        return (y, s % 2, x, 2 * zl + s // 2, c)

    return table(move)


CORE = table(lambda x, zl, y, zh, c: (x, zl, y, zh, 1 - c))
ALONG_X = [
    [table(lambda x, zl, y, zh, c, i=i, j=j: ((x + i) % 4, zl ^ j, y, zh, c)) for j in range(2)] for i in range(4)
]
ALONG_Y = [table(lambda x, zl, y, zh, c, k=k: (x, zl, (y + k) % 4, zh, c)) for k in range(4)]
OWNER = [to_owner(k) for k in range(4)]
HOLDER = table(lambda x, zl, y, zh, c: (y, zh // 2, x, 2 * (zh % 2) + zl, c))
Z_GROUPS = [[8 * y + 2 * z + c for z in range(4)] for y in range(4) for c in range(2)]


def send(array, pairs):
    return lax.ppermute(array, AXES, pairs)


def after(array, *others):
    return lax.optimization_barrier((array,) + others)[0]


def exchange(array, axis, groups=None):
    return lax.all_to_all(array, axis, split_axis=0, concat_axis=0, tiled=True, axis_index_groups=groups)


def copies(array, size):
    return jnp.broadcast_to(array[None], (size,) + array.shape)


def highest(array):
    return jnp.max(jnp.abs(array), keepdims=True).reshape(1, 1).astype(jnp.float32)


def weight_kernel(at_ref, first_ref, second_ref, third_ref, fourth_ref, columns_ref, out_ref):
    total = None
    for k, block_ref in enumerate((first_ref, second_ref, third_ref, fourth_ref)):
        term = lax.dot_general(
            block_ref[0], columns_ref[at_ref[k]], COLUMNS_BY_COLUMNS, preferred_element_type=jnp.float32
        )
        total = term if total is None else total + term
    out_ref[...] = total.reshape(out_ref.shape)


def fill_kernel(core_ref, values_ref, whole_ref, out_ref):
    out_ref[...] = values_ref[...].reshape(out_ref.shape)


def weight_part(at, blocks, columns, place=None):
    halves, rows, width = blocks[0].shape
    block = pl.BlockSpec((1, rows, width), lambda i, at: (i, 0, 0))
    if place is None:
        out_shape = jax.ShapeDtypeStruct((halves, width, width), jnp.float32)
        out_spec = pl.BlockSpec((1, width, width), lambda i, at: (i, 0, 0))
    else:
        out_shape = jax.ShapeDtypeStruct((halves, 2, width, width), jnp.float32)
        out_spec = pl.BlockSpec((1, 1, width, width), lambda i, at: (i, at[4], 0, 0))
    return pl.pallas_call(
        weight_kernel,
        out_shape=out_shape,
        grid_spec=pltpu.PrefetchScalarGridSpec(
            num_scalar_prefetch=1,
            grid=(halves,),
            in_specs=[block] * 4 + [pl.BlockSpec(columns.shape, lambda i, at: (0, 0, 0))],
            out_specs=out_spec,
        ),
        compiler_params=pltpu.CompilerParams(vmem_limit_bytes=32 * 1024 * 1024),
        cost_estimate=pl.CostEstimate(
            flops=8 * halves * rows * width * width, bytes_accessed=8 * halves * rows * width, transcendentals=0
        ),
    )(at, *blocks, columns)


def fill(core, values, whole):
    halves, width, _ = values.shape
    return pl.pallas_call(
        fill_kernel,
        out_shape=jax.ShapeDtypeStruct(whole.shape, whole.dtype),
        grid_spec=pltpu.PrefetchScalarGridSpec(
            num_scalar_prefetch=1,
            grid=(halves,),
            in_specs=[
                pl.BlockSpec((1, width, width), lambda i, core: (i, 0, 0)),
                pl.BlockSpec(memory_space=pl.ANY),
            ],
            out_specs=pl.BlockSpec((1, 1, width, width), lambda i, core: (i, core[0], 0, 0)),
        ),
        input_output_aliases={2: 0},
        compiler_params=pltpu.CompilerParams(vmem_limit_bytes=32 * 1024 * 1024),
    )(core, values, whole)


def body(hidden_in, ln_gain, ln_bias, q_weight, grad_query):
    tokens, width = hidden_in.shape
    d, t = lax.axis_index("dp"), lax.axis_index("tensor")
    x, zl, y, zh, c = d // 2, d % 2, t // 8, (t // 2) % 4, t % 2
    features = width * TENSOR

    there = send(grad_query, ALONG_X[0][1])
    pair = jnp.where(zl == 0, jnp.concatenate([grad_query, there]), jnp.concatenate([there, grad_query]))
    query = jnp.stack([pair] + [send(pair, ALONG_X[i][0]) for i in (1, 2, 3)])

    values = hidden_in.astype(jnp.float32)
    told = jnp.concatenate([jnp.sum(values, axis=1), jnp.sum(values * values, axis=1)])
    told = exchange(copies(after(told, there), TENSOR), "tensor")
    query, told = lax.optimization_barrier((query, told))
    sums = jnp.sum(told, axis=0) / features
    row_mean = sums[:tokens, None]
    inv_std = lax.rsqrt(sums[tokens:, None] - row_mean * row_mean + 1e-05)
    standard = (values - row_mean) * inv_std
    normed = (standard * ln_gain + ln_bias).astype(jnp.bfloat16)

    quarters = q_weight.reshape(2, 2, width, width)
    mine = lax.dynamic_index_in_dim(quarters, c, axis=1, keepdims=False).reshape(2 * width, width)
    theirs = lax.dynamic_index_in_dim(quarters, 1 - c, axis=1, keepdims=False).reshape(2 * width, width)
    theirs = send(theirs, CORE)
    query_other = send(query, CORE)
    bound = width * highest(query) * highest(q_weight)
    bound = bound + send(bound, CORE)
    power = jnp.clip(jnp.floor(jnp.log2(CAP / bound)), -100.0, 100.0)

    at = [(x - y - k) % 4 for k in range(4)]
    own_tokens = [lax.dynamic_index_in_dim(query, at[k], axis=0, keepdims=False) for k in range(4)]
    other_tokens = [lax.dynamic_index_in_dim(query_other, at[k], axis=0, keepdims=False) for k in range(4)]

    extended = 2 * tokens + 16
    last = lax.broadcasted_iota(jnp.int32, (extended, 2 * width), 0) >= 2 * tokens
    longer = lambda array: jnp.pad(array, ((0, 16), (0, 0)))
    sent, received = [], []
    for k in (2, 1, 3, 0):
        part = lax.dot_general(
            longer(own_tokens[k]), mine, ROWS_BY_ROWS, preferred_element_type=jnp.float32
        ) + lax.dot_general(longer(other_tokens[k]), theirs, ROWS_BY_ROWS, preferred_element_type=jnp.float32)
        sent.append(jnp.where(last, power, part * jnp.exp2(power)).astype(jnp.float16))
        received.append(send(sent[-1], ALONG_Y[k]) if k else sent[-1])


    normed = send(after(normed, *sent), HOLDER)
    *received, normed = lax.optimization_barrier((*received, normed))

    powers = jnp.stack([message[2 * tokens :, :width] for message in received]).astype(jnp.float32)
    power = jnp.min(powers, axis=0) - 2.0
    scales = jnp.exp2(power - powers)
    pieces = []
    for k in range(4):
        s = (zh + k) % 4
        cut = ((s % 2) * tokens, (s // 2) * width)
        piece = sum(
            lax.dynamic_slice(message, cut, (tokens, width)).astype(jnp.float32) * scales[i, :1]
            for i, message in enumerate(received)
        )
        pieces.append(jnp.concatenate([piece, power]).astype(jnp.float16))
    pieces = [send(piece, OWNER[k]) for k, piece in enumerate(pieces)]

    block = exchange(copies(normed, 4), "tensor", Z_GROUPS).reshape(2, 2 * tokens, width)
    pieces, block = lax.optimization_barrier((pieces, block))
    blocks = [block] + [send(block, ALONG_Y[k]) for k in (1, 2, 3)]

    scales = jnp.exp2(-jnp.stack([piece[tokens:] for piece in pieces]).astype(jnp.float32))
    grad_normed = sum(piece[:tokens].astype(jnp.float32) * scales[i, :1] for i, piece in enumerate(pieces))

    scaled = grad_normed * ln_gain
    told = jnp.concatenate([jnp.sum(scaled, axis=1), jnp.sum(scaled * standard, axis=1)])
    told = exchange(copies(told, TENSOR), "tensor")
    sums = jnp.stack([jnp.sum(grad_normed * standard, axis=0), jnp.sum(grad_normed, axis=0)])
    others = [send(sums, ALONG_X[i][0]) for i in (1, 2, 3)]
    told, others, blocks = lax.optimization_barrier((told, others, blocks))
    sums = sums + others[0] + others[1] + others[2]
    sums = sums + send(sums, ALONG_X[0][1])
    told = jnp.sum(told, axis=0) / features
    grad_input = inv_std * (scaled - told[:tokens, None] - standard * told[tokens:, None])

    at = jnp.stack([(x - y + k) % 4 for k in range(4)] + [c]).astype(jnp.int32)
    grad_other = send(weight_part(at, blocks, query_other), CORE)
    grad_mine = weight_part(at, blocks, query, c)
    grad_weight = fill((1 - c).astype(jnp.int32).reshape(1), grad_other, grad_mine).reshape(4 * width, width)
    return (grad_input, grad_weight, sums[0], sums[1])


def solution(mesh):
    placed = (P("dp", "tensor"), P("tensor"), P("tensor"), P("dp", "tensor"), P("dp", "tensor"))
    return jax.shard_map(
        body,
        mesh=mesh,
        in_specs=placed,
        out_specs=(P("dp", "tensor"), P("dp", "tensor"), P("tensor"), P("tensor")),
        check_vma=False,
    )
```

```python
import jax
import jax.numpy as jnp
from jax import lax
from jax.experimental import pallas as pl
from jax.experimental.pallas import tpu as pltpu
from jax.sharding import PartitionSpec as P

AXES = ("dp", "tensor")
DATA, TENSOR = 8, 32
CAP = 32768.0
ROWS_BY_ROWS = (((1,), (1,)), ((), ()))
COLUMNS_BY_COLUMNS = (((0,), (0,)), ((), ()))


def flat(x, zl, y, zh, c):
    return ((x * 2 + zl) * 4 + y) * 8 + zh * 2 + c


def table(move):
    pairs = []
    for d in range(DATA):
        for t in range(TENSOR):
            place = (d // 2, d % 2, t // 8, (t // 2) % 4, t % 2)
            pairs.append((flat(*place), flat(*move(*place))))
    return pairs


CORE = table(lambda x, zl, y, zh, c: (x, zl, y, zh, 1 - c))
ALONG_X = [
    [table(lambda x, zl, y, zh, c, i=i, j=j: ((x + i) % 4, zl ^ j, y, zh, c)) for j in range(2)] for i in range(4)
]
ALONG_Y = [table(lambda x, zl, y, zh, c, k=k: (x, zl, (y + k) % 4, zh, c)) for k in range(4)]
ALONG_Z = [table(lambda x, zl, y, zh, c, k=k: (x, zl, y, (zh + k) % 4, c)) for k in range(4)]
HOLDER = table(lambda x, zl, y, zh, c: (y, zh // 2, x, 2 * (zh % 2) + zl, c))
OWNER = [(b, a) for a, b in HOLDER]
Z_GROUPS = [[8 * y + 2 * z + c for z in range(4)] for y in range(4) for c in range(2)]


def send(array, pairs):
    return lax.ppermute(array, AXES, pairs)


def after(array, *others):
    return lax.optimization_barrier((array,) + others)[0]


def exchange(array, axis, groups=None):
    return lax.all_to_all(array, axis, split_axis=0, concat_axis=0, tiled=True, axis_index_groups=groups)


def copies(array, size):
    return jnp.broadcast_to(array[None], (size,) + array.shape)


def highest(array):
    return jnp.max(jnp.abs(array), keepdims=True).reshape(1, 1).astype(jnp.float32)


def weight_kernel(at_ref, first_ref, second_ref, third_ref, fourth_ref, columns_ref, out_ref):
    total = None
    for k, block_ref in enumerate((first_ref, second_ref, third_ref, fourth_ref)):
        term = lax.dot_general(
            block_ref[0], columns_ref[at_ref[k]], COLUMNS_BY_COLUMNS, preferred_element_type=jnp.float32
        )
        total = term if total is None else total + term
    out_ref[...] = total.reshape(out_ref.shape)


def fill_kernel(core_ref, values_ref, whole_ref, out_ref):
    out_ref[...] = values_ref[...].reshape(out_ref.shape)


def weight_part(at, blocks, columns, place=None):
    halves, rows, width = blocks[0].shape
    block = pl.BlockSpec((1, rows, width), lambda i, at: (i, 0, 0))
    if place is None:
        out_shape = jax.ShapeDtypeStruct((halves, width, width), jnp.float32)
        out_spec = pl.BlockSpec((1, width, width), lambda i, at: (i, 0, 0))
    else:
        out_shape = jax.ShapeDtypeStruct((halves, 2, width, width), jnp.float32)
        out_spec = pl.BlockSpec((1, 1, width, width), lambda i, at: (i, at[4], 0, 0))
    return pl.pallas_call(
        weight_kernel,
        out_shape=out_shape,
        grid_spec=pltpu.PrefetchScalarGridSpec(
            num_scalar_prefetch=1,
            grid=(halves,),
            in_specs=[block] * 4 + [pl.BlockSpec(columns.shape, lambda i, at: (0, 0, 0))],
            out_specs=out_spec,
        ),
        compiler_params=pltpu.CompilerParams(vmem_limit_bytes=32 * 1024 * 1024),
        cost_estimate=pl.CostEstimate(
            flops=8 * halves * rows * width * width, bytes_accessed=8 * halves * rows * width, transcendentals=0
        ),
    )(at, *blocks, columns)


def fill(core, values, whole):
    halves, width, _ = values.shape
    return pl.pallas_call(
        fill_kernel,
        out_shape=jax.ShapeDtypeStruct(whole.shape, whole.dtype),
        grid_spec=pltpu.PrefetchScalarGridSpec(
            num_scalar_prefetch=1,
            grid=(halves,),
            in_specs=[
                pl.BlockSpec((1, width, width), lambda i, core: (i, 0, 0)),
                pl.BlockSpec(memory_space=pl.ANY),
            ],
            out_specs=pl.BlockSpec((1, 1, width, width), lambda i, core: (i, core[0], 0, 0)),
        ),
        input_output_aliases={2: 0},
        compiler_params=pltpu.CompilerParams(vmem_limit_bytes=32 * 1024 * 1024),
    )(core, values, whole)


def body(hidden_in, ln_gain, ln_bias, q_weight, grad_query):
    tokens, width = hidden_in.shape
    d, t = lax.axis_index("dp"), lax.axis_index("tensor")
    x, zl, y, zh, c = d // 2, d % 2, t // 8, (t // 2) % 4, t % 2
    features = width * TENSOR

    there = send(grad_query, ALONG_X[0][1])
    pair = jnp.where(zl == 0, jnp.concatenate([grad_query, there]), jnp.concatenate([there, grad_query]))
    query = jnp.stack([pair] + [send(pair, ALONG_X[i][0]) for i in (1, 2, 3)])

    values = hidden_in.astype(jnp.float32)
    told = jnp.concatenate([jnp.sum(values, axis=1), jnp.sum(values * values, axis=1)])
    told = exchange(copies(after(told, there), TENSOR), "tensor")
    query, told = lax.optimization_barrier((query, told))
    sums = jnp.sum(told, axis=0) / features
    row_mean = sums[:tokens, None]
    inv_std = lax.rsqrt(sums[tokens:, None] - row_mean * row_mean + 1e-05)
    standard = (values - row_mean) * inv_std
    normed = (standard * ln_gain + ln_bias).astype(jnp.bfloat16)

    quarters = q_weight.reshape(2, 2, width, width)
    mine = lax.dynamic_index_in_dim(quarters, c, axis=1, keepdims=False).reshape(2 * width, width)
    theirs = lax.dynamic_index_in_dim(quarters, 1 - c, axis=1, keepdims=False).reshape(2 * width, width)
    theirs = send(theirs, CORE)
    query_other = send(query, CORE)
    bound = width * highest(query) * highest(q_weight)
    bound = bound + send(bound, CORE)
    power = jnp.clip(jnp.floor(jnp.log2(CAP / bound)), -100.0, 100.0)

    at = [(x - y - k) % 4 for k in range(4)]
    own_tokens = [lax.dynamic_index_in_dim(query, at[k], axis=0, keepdims=False) for k in range(4)]
    other_tokens = [lax.dynamic_index_in_dim(query_other, at[k], axis=0, keepdims=False) for k in range(4)]

    extended = 2 * tokens + 16
    last = lax.broadcasted_iota(jnp.int32, (extended, 2 * width), 0) >= 2 * tokens
    longer = lambda array: jnp.pad(array, ((0, 16), (0, 0)))
    sent, received = [], []
    for k in (2, 1, 3, 0):
        part = lax.dot_general(
            longer(own_tokens[k]), mine, ROWS_BY_ROWS, preferred_element_type=jnp.float32
        ) + lax.dot_general(longer(other_tokens[k]), theirs, ROWS_BY_ROWS, preferred_element_type=jnp.float32)
        sent.append(jnp.where(last, power, part * jnp.exp2(power)).astype(jnp.float16))
        received.append(send(sent[-1], ALONG_Y[k]) if k else sent[-1])


    normed = send(after(normed, *sent), HOLDER)
    *received, normed = lax.optimization_barrier((*received, normed))

    powers = jnp.stack([message[2 * tokens :, :width] for message in received]).astype(jnp.float32)
    power = jnp.min(powers, axis=0) - 2.0
    scales = jnp.exp2(power - powers)
    pieces = []
    for k in range(4):
        s = (zh + k) % 4
        cut = ((s % 2) * tokens, (s // 2) * width)
        piece = sum(
            lax.dynamic_slice(message, cut, (tokens, width)).astype(jnp.float32) * scales[i, :1]
            for i, message in enumerate(received)
        )
        pieces.append(jnp.concatenate([piece, power]).astype(jnp.float16))
    pieces = [send(piece, ALONG_Z[k]) if k else piece for k, piece in enumerate(pieces)]

    block = exchange(copies(normed, 4), "tensor", Z_GROUPS).reshape(2, 2 * tokens, width)
    blocks = [block] + [send(block, ALONG_Y[k]) for k in (1, 2, 3)]

    powers = jnp.stack([piece[tokens:] for piece in pieces]).astype(jnp.float32)
    power = jnp.min(powers, axis=0) - 2.0
    scales = jnp.exp2(power - powers)
    piece = sum(piece[:tokens].astype(jnp.float32) * scales[i, :1] for i, piece in enumerate(pieces))
    piece = send(jnp.concatenate([piece, power]).astype(jnp.float16), OWNER)
    grad_normed = piece[:tokens].astype(jnp.float32) * jnp.exp2(-piece[tokens : tokens + 1].astype(jnp.float32))

    scaled = grad_normed * ln_gain
    told = jnp.concatenate([jnp.sum(scaled, axis=1), jnp.sum(scaled * standard, axis=1)])
    told = exchange(copies(told, TENSOR), "tensor")
    sums = jnp.stack([jnp.sum(grad_normed * standard, axis=0), jnp.sum(grad_normed, axis=0)])
    others = [send(sums, ALONG_X[i][0]) for i in (1, 2, 3)]
    at = jnp.stack([(x - y + k) % 4 for k in range(4)] + [c]).astype(jnp.int32)
    grad_other = weight_part(at, blocks, query_other)
    grad_mine = weight_part(at, blocks, query, c)
    told, others, grad_other, grad_mine = lax.optimization_barrier((told, others, grad_other, grad_mine))
    grad_other = send(grad_other, CORE)
    sums = sums + others[0] + others[1] + others[2]
    sums = sums + send(sums, ALONG_X[0][1])
    told = jnp.sum(told, axis=0) / features
    grad_input = inv_std * (scaled - told[:tokens, None] - standard * told[tokens:, None])

    grad_weight = fill((1 - c).astype(jnp.int32).reshape(1), grad_other, grad_mine).reshape(4 * width, width)
    return (grad_input, grad_weight, sums[0], sums[1])


def solution(mesh):
    placed = (P("dp", "tensor"), P("tensor"), P("tensor"), P("dp", "tensor"), P("dp", "tensor"))
    return jax.shard_map(
        body,
        mesh=mesh,
        in_specs=placed,
        out_specs=(P("dp", "tensor"), P("dp", "tensor"), P("tensor"), P("tensor")),
        check_vma=False,
    )
```

```python
import jax
import jax.numpy as jnp
from jax import lax
from jax.experimental import pallas as pl
from jax.experimental.pallas import tpu as pltpu
from jax.sharding import PartitionSpec as P

AXES = ("dp", "tensor")
DATA, TENSOR = 8, 32
CAP = 32768.0
ROWS_BY_ROWS = (((1,), (1,)), ((), ()))
COLUMNS_BY_COLUMNS = (((0,), (0,)), ((), ()))


def flat(x, zl, y, zh, c):
    return ((x * 2 + zl) * 4 + y) * 8 + zh * 2 + c


def table(move):
    pairs = []
    for d in range(DATA):
        for t in range(TENSOR):
            place = (d // 2, d % 2, t // 8, (t // 2) % 4, t % 2)
            pairs.append((flat(*place), flat(*move(*place))))
    return pairs


CORE = table(lambda x, zl, y, zh, c: (x, zl, y, zh, 1 - c))
ALONG_X = [
    [table(lambda x, zl, y, zh, c, i=i, j=j: ((x + i) % 4, zl ^ j, y, zh, c)) for j in range(2)] for i in range(4)
]
ALONG_Y = [table(lambda x, zl, y, zh, c, k=k: (x, zl, (y + k) % 4, zh, c)) for k in range(4)]
ALONG_Z = [table(lambda x, zl, y, zh, c, k=k: (x, zl, y, (zh + k) % 4, c)) for k in range(4)]
HOLDER = table(lambda x, zl, y, zh, c: (y, zh // 2, x, 2 * (zh % 2) + zl, c))
OWNER = [(b, a) for a, b in HOLDER]
Z_GROUPS = [[8 * y + 2 * z + c for z in range(4)] for y in range(4) for c in range(2)]


def send(array, pairs):
    return lax.ppermute(array, AXES, pairs)


def after(array, *others):
    return lax.optimization_barrier((array,) + others)[0]


def exchange(array, axis, groups=None):
    return lax.all_to_all(array, axis, split_axis=0, concat_axis=0, tiled=True, axis_index_groups=groups)


def copies(array, size):
    return jnp.broadcast_to(array[None], (size,) + array.shape)


def highest(array):
    return jnp.max(jnp.abs(array), keepdims=True).reshape(1, 1).astype(jnp.float32)


def weight_kernel(at_ref, first_ref, second_ref, third_ref, fourth_ref, columns_ref, out_ref):
    total = None
    for k, block_ref in enumerate((first_ref, second_ref, third_ref, fourth_ref)):
        term = lax.dot_general(
            block_ref[0], columns_ref[at_ref[k]], COLUMNS_BY_COLUMNS, preferred_element_type=jnp.float32
        )
        total = term if total is None else total + term
    out_ref[...] = total.reshape(out_ref.shape)


def fill_kernel(core_ref, values_ref, whole_ref, out_ref):
    out_ref[...] = values_ref[...].reshape(out_ref.shape)


def weight_part(at, blocks, columns, place=None):
    halves, rows, width = blocks[0].shape
    block = pl.BlockSpec((1, rows, width), lambda i, at: (i, 0, 0))
    if place is None:
        out_shape = jax.ShapeDtypeStruct((halves, width, width), jnp.float32)
        out_spec = pl.BlockSpec((1, width, width), lambda i, at: (i, 0, 0))
    else:
        out_shape = jax.ShapeDtypeStruct((halves, 2, width, width), jnp.float32)
        out_spec = pl.BlockSpec((1, 1, width, width), lambda i, at: (i, at[4], 0, 0))
    return pl.pallas_call(
        weight_kernel,
        out_shape=out_shape,
        grid_spec=pltpu.PrefetchScalarGridSpec(
            num_scalar_prefetch=1,
            grid=(halves,),
            in_specs=[block] * 4 + [pl.BlockSpec(columns.shape, lambda i, at: (0, 0, 0))],
            out_specs=out_spec,
        ),
        compiler_params=pltpu.CompilerParams(vmem_limit_bytes=32 * 1024 * 1024),
        cost_estimate=pl.CostEstimate(
            flops=8 * halves * rows * width * width, bytes_accessed=8 * halves * rows * width, transcendentals=0
        ),
    )(at, *blocks, columns)


def fill(core, values, whole):
    halves, width, _ = values.shape
    return pl.pallas_call(
        fill_kernel,
        out_shape=jax.ShapeDtypeStruct(whole.shape, whole.dtype),
        grid_spec=pltpu.PrefetchScalarGridSpec(
            num_scalar_prefetch=1,
            grid=(halves,),
            in_specs=[
                pl.BlockSpec((1, width, width), lambda i, core: (i, 0, 0)),
                pl.BlockSpec(memory_space=pl.ANY),
            ],
            out_specs=pl.BlockSpec((1, 1, width, width), lambda i, core: (i, core[0], 0, 0)),
        ),
        input_output_aliases={2: 0},
        compiler_params=pltpu.CompilerParams(vmem_limit_bytes=32 * 1024 * 1024),
    )(core, values, whole)


def body(hidden_in, ln_gain, ln_bias, q_weight, grad_query):
    tokens, width = hidden_in.shape
    d, t = lax.axis_index("dp"), lax.axis_index("tensor")
    x, zl, y, zh, c = d // 2, d % 2, t // 8, (t // 2) % 4, t % 2
    features = width * TENSOR

    there = send(grad_query, ALONG_X[0][1])
    pair = jnp.where(zl == 0, jnp.concatenate([grad_query, there]), jnp.concatenate([there, grad_query]))
    query = jnp.stack([pair] + [send(pair, ALONG_X[i][0]) for i in (1, 2, 3)])

    values = hidden_in.astype(jnp.float32)
    told = jnp.concatenate([jnp.sum(values, axis=1), jnp.sum(values * values, axis=1)] * 4)
    told = exchange(copies(after(told, there), TENSOR), "tensor")
    sums = jnp.sum(told[:, : 2 * tokens], axis=0) / features
    row_mean = sums[:tokens, None]
    inv_std = lax.rsqrt(sums[tokens:, None] - row_mean * row_mean + 1e-05)
    standard = (values - row_mean) * inv_std
    normed = (standard * ln_gain + ln_bias).astype(jnp.bfloat16)

    quarters = q_weight.reshape(2, 2, width, width)
    mine = lax.dynamic_index_in_dim(quarters, c, axis=1, keepdims=False).reshape(2 * width, width)
    theirs = lax.dynamic_index_in_dim(quarters, 1 - c, axis=1, keepdims=False).reshape(2 * width, width)
    theirs = send(theirs, CORE)
    query_other = send(query, CORE)
    bound = width * highest(query) * highest(q_weight)
    bound = bound + send(bound, CORE)
    power = jnp.clip(jnp.floor(jnp.log2(CAP / bound)), -100.0, 100.0)

    at = [(x - y - k) % 4 for k in range(4)]
    own_tokens = [lax.dynamic_index_in_dim(query, at[k], axis=0, keepdims=False) for k in range(4)]
    other_tokens = [lax.dynamic_index_in_dim(query_other, at[k], axis=0, keepdims=False) for k in range(4)]

    extended = 2 * tokens + 16
    last = lax.broadcasted_iota(jnp.int32, (extended, 2 * width), 0) >= 2 * tokens
    longer = lambda array: jnp.pad(array, ((0, 16), (0, 0)))
    sent, received = [], []
    for k in (2, 1, 3, 0):
        part = lax.dot_general(
            longer(own_tokens[k]), mine, ROWS_BY_ROWS, preferred_element_type=jnp.float32
        ) + lax.dot_general(longer(other_tokens[k]), theirs, ROWS_BY_ROWS, preferred_element_type=jnp.float32)
        sent.append(jnp.where(last, power, part * jnp.exp2(power)).astype(jnp.float16))
        received.append(send(sent[-1], ALONG_Y[k]) if k else sent[-1])


    normed = send(after(normed, *sent), HOLDER)
    *received, normed = lax.optimization_barrier((*received, normed))

    powers = jnp.stack([message[2 * tokens :, :width] for message in received]).astype(jnp.float32)
    power = jnp.min(powers, axis=0) - 2.0
    scales = jnp.exp2(power - powers)
    pieces = []
    for k in range(4):
        s = (zh + k) % 4
        cut = ((s % 2) * tokens, (s // 2) * width)
        piece = sum(
            lax.dynamic_slice(message, cut, (tokens, width)).astype(jnp.float32) * scales[i, :1]
            for i, message in enumerate(received)
        )
        pieces.append(jnp.concatenate([piece, power]).astype(jnp.float16))
    pieces = [send(piece, ALONG_Z[k]) if k else piece for k, piece in enumerate(pieces)]

    block = exchange(copies(normed, 4), "tensor", Z_GROUPS).reshape(2, 2 * tokens, width)
    blocks = [block] + [send(block, ALONG_Y[k]) for k in (1, 2, 3)]

    powers = jnp.stack([piece[tokens:] for piece in pieces]).astype(jnp.float32)
    power = jnp.min(powers, axis=0) - 2.0
    scales = jnp.exp2(power - powers)
    piece = sum(piece[:tokens].astype(jnp.float32) * scales[i, :1] for i, piece in enumerate(pieces))
    piece = send(jnp.concatenate([piece, power]).astype(jnp.float16), OWNER)
    grad_normed = piece[:tokens].astype(jnp.float32) * jnp.exp2(-piece[tokens : tokens + 1].astype(jnp.float32))

    scaled = grad_normed * ln_gain
    told = jnp.concatenate([jnp.sum(scaled, axis=1), jnp.sum(scaled * standard, axis=1)])
    told = exchange(copies(told, TENSOR), "tensor")
    sums = jnp.stack([jnp.sum(grad_normed * standard, axis=0), jnp.sum(grad_normed, axis=0)])
    others = [send(sums, ALONG_X[i][0]) for i in (1, 2, 3)]
    at = jnp.stack([(x - y + k) % 4 for k in range(4)] + [c]).astype(jnp.int32)
    grad_other = weight_part(at, blocks, query_other)
    grad_mine = weight_part(at, blocks, query, c)
    told, others, grad_other, grad_mine = lax.optimization_barrier((told, others, grad_other, grad_mine))
    grad_other = send(grad_other, CORE)
    sums = sums + others[0] + others[1] + others[2]
    sums = sums + send(sums, ALONG_X[0][1])
    told = jnp.sum(told, axis=0) / features
    grad_input = inv_std * (scaled - told[:tokens, None] - standard * told[tokens:, None])

    grad_weight = fill((1 - c).astype(jnp.int32).reshape(1), grad_other, grad_mine).reshape(4 * width, width)
    return (grad_input, grad_weight, sums[0], sums[1])


def solution(mesh):
    placed = (P("dp", "tensor"), P("tensor"), P("tensor"), P("dp", "tensor"), P("dp", "tensor"))
    return jax.shard_map(
        body,
        mesh=mesh,
        in_specs=placed,
        out_specs=(P("dp", "tensor"), P("dp", "tensor"), P("tensor"), P("tensor")),
        check_vma=False,
    )
```

```python
import jax
import jax.numpy as jnp
from jax import lax
from jax.experimental import pallas as pl
from jax.experimental.pallas import tpu as pltpu
from jax.sharding import PartitionSpec as P

AXES = ("dp", "tensor")
DATA, TENSOR = 8, 32
CAP = 32768.0
ROWS_BY_ROWS = (((1,), (1,)), ((), ()))
COLUMNS_BY_COLUMNS = (((0,), (0,)), ((), ()))


def flat(x, zl, y, zh, c):
    return ((x * 2 + zl) * 4 + y) * 8 + zh * 2 + c


def table(move):
    pairs = []
    for d in range(DATA):
        for t in range(TENSOR):
            place = (d // 2, d % 2, t // 8, (t // 2) % 4, t % 2)
            pairs.append((flat(*place), flat(*move(*place))))
    return pairs


CORE = table(lambda x, zl, y, zh, c: (x, zl, y, zh, 1 - c))
ALONG_X = [
    [table(lambda x, zl, y, zh, c, i=i, j=j: ((x + i) % 4, zl ^ j, y, zh, c)) for j in range(2)] for i in range(4)
]
ALONG_Y = [table(lambda x, zl, y, zh, c, k=k: (x, zl, (y + k) % 4, zh, c)) for k in range(4)]
ALONG_Z = [table(lambda x, zl, y, zh, c, k=k: (x, zl, y, (zh + k) % 4, c)) for k in range(4)]
HOLDER = table(lambda x, zl, y, zh, c: (y, zh // 2, x, 2 * (zh % 2) + zl, c))
OWNER = [(b, a) for a, b in HOLDER]
Z_GROUPS = [[8 * y + 2 * z + c for z in range(4)] for y in range(4) for c in range(2)]


def send(array, pairs):
    return lax.ppermute(array, AXES, pairs)


def after(array, *others):
    return lax.optimization_barrier((array,) + others)[0]


def exchange(array, axis, groups=None):
    return lax.all_to_all(array, axis, split_axis=0, concat_axis=0, tiled=True, axis_index_groups=groups)


def copies(array, size):
    return jnp.broadcast_to(array[None], (size,) + array.shape)


def highest(array):
    return jnp.max(jnp.abs(array), keepdims=True).reshape(1, 1).astype(jnp.float32)


def weight_kernel(at_ref, first_ref, second_ref, third_ref, fourth_ref, columns_ref, out_ref):
    total = None
    for k, block_ref in enumerate((first_ref, second_ref, third_ref, fourth_ref)):
        term = lax.dot_general(
            block_ref[0], columns_ref[at_ref[k]], COLUMNS_BY_COLUMNS, preferred_element_type=jnp.float32
        )
        total = term if total is None else total + term
    out_ref[...] = total.reshape(out_ref.shape)


def fill_kernel(core_ref, values_ref, whole_ref, out_ref):
    out_ref[...] = values_ref[...].reshape(out_ref.shape)


def weight_part(at, blocks, columns, place=None):
    halves, rows, width = blocks[0].shape
    block = pl.BlockSpec((1, rows, width), lambda i, at: (i, 0, 0))
    if place is None:
        out_shape = jax.ShapeDtypeStruct((halves, width, width), jnp.float32)
        out_spec = pl.BlockSpec((1, width, width), lambda i, at: (i, 0, 0))
    else:
        out_shape = jax.ShapeDtypeStruct((halves, 2, width, width), jnp.float32)
        out_spec = pl.BlockSpec((1, 1, width, width), lambda i, at: (i, at[4], 0, 0))
    return pl.pallas_call(
        weight_kernel,
        out_shape=out_shape,
        grid_spec=pltpu.PrefetchScalarGridSpec(
            num_scalar_prefetch=1,
            grid=(halves,),
            in_specs=[block] * 4 + [pl.BlockSpec(columns.shape, lambda i, at: (0, 0, 0))],
            out_specs=out_spec,
        ),
        compiler_params=pltpu.CompilerParams(vmem_limit_bytes=32 * 1024 * 1024),
        cost_estimate=pl.CostEstimate(
            flops=8 * halves * rows * width * width, bytes_accessed=8 * halves * rows * width, transcendentals=0
        ),
    )(at, *blocks, columns)


def fill(core, values, whole):
    halves, width, _ = values.shape
    return pl.pallas_call(
        fill_kernel,
        out_shape=jax.ShapeDtypeStruct(whole.shape, whole.dtype),
        grid_spec=pltpu.PrefetchScalarGridSpec(
            num_scalar_prefetch=1,
            grid=(halves,),
            in_specs=[
                pl.BlockSpec((1, width, width), lambda i, core: (i, 0, 0)),
                pl.BlockSpec(memory_space=pl.ANY),
            ],
            out_specs=pl.BlockSpec((1, 1, width, width), lambda i, core: (i, core[0], 0, 0)),
        ),
        input_output_aliases={2: 0},
        compiler_params=pltpu.CompilerParams(vmem_limit_bytes=32 * 1024 * 1024),
    )(core, values, whole)


def body(hidden_in, ln_gain, ln_bias, q_weight, grad_query):
    tokens, width = hidden_in.shape
    d, t = lax.axis_index("dp"), lax.axis_index("tensor")
    x, zl, y, zh, c = d // 2, d % 2, t // 8, (t // 2) % 4, t % 2
    features = width * TENSOR

    there = send(grad_query, ALONG_X[0][1])
    pair = jnp.where(zl == 0, jnp.concatenate([grad_query, there]), jnp.concatenate([there, grad_query]))
    query = jnp.stack([pair] + [send(pair, ALONG_X[i][0]) for i in (1, 2, 3)])

    values = hidden_in.astype(jnp.float32)
    told = jnp.concatenate([jnp.sum(values, axis=1), jnp.sum(values * values, axis=1)] * 4)
    told = exchange(copies(after(told, there), TENSOR), "tensor")
    sums = jnp.sum(told[:, : 2 * tokens], axis=0) / features
    row_mean = sums[:tokens, None]
    inv_std = lax.rsqrt(sums[tokens:, None] - row_mean * row_mean + 1e-05)
    standard = (values - row_mean) * inv_std
    normed = (standard * ln_gain + ln_bias).astype(jnp.bfloat16)

    quarters = q_weight.reshape(2, 2, width, width)
    mine = lax.dynamic_index_in_dim(quarters, c, axis=1, keepdims=False).reshape(2 * width, width)
    theirs = lax.dynamic_index_in_dim(quarters, 1 - c, axis=1, keepdims=False).reshape(2 * width, width)
    theirs = send(theirs, CORE)
    query_other = send(query, CORE)
    bound = width * highest(query) * highest(q_weight)
    bound = bound + send(bound, CORE)
    power = jnp.clip(jnp.floor(jnp.log2(CAP / bound)), -100.0, 100.0)

    at = [(x - y - k) % 4 for k in range(4)]
    own_tokens = [lax.dynamic_index_in_dim(query, at[k], axis=0, keepdims=False) for k in range(4)]
    other_tokens = [lax.dynamic_index_in_dim(query_other, at[k], axis=0, keepdims=False) for k in range(4)]

    extended = 2 * tokens + 16
    last = lax.broadcasted_iota(jnp.int32, (extended, 2 * width), 0) >= 2 * tokens
    longer = lambda array: jnp.pad(array, ((0, 16), (0, 0)))
    sent, received = [], []
    for k in (1, 3, 2, 0):
        part = lax.dot_general(
            longer(own_tokens[k]), mine, ROWS_BY_ROWS, preferred_element_type=jnp.float32
        ) + lax.dot_general(longer(other_tokens[k]), theirs, ROWS_BY_ROWS, preferred_element_type=jnp.float32)
        sent.append(jnp.where(last, power, part * jnp.exp2(power)).astype(jnp.float16))
        received.append(send(sent[-1], ALONG_Y[k]) if k else sent[-1])


    normed = send(after(normed, *sent), HOLDER)
    *received, normed = lax.optimization_barrier((*received, normed))

    powers = jnp.stack([message[2 * tokens :, :width] for message in received]).astype(jnp.float32)
    power = jnp.min(powers, axis=0) - 2.0
    scales = jnp.exp2(power - powers)
    pieces = []
    for k in range(4):
        s = (zh + k) % 4
        cut = ((s % 2) * tokens, (s // 2) * width)
        piece = sum(
            lax.dynamic_slice(message, cut, (tokens, width)).astype(jnp.float32) * scales[i, :1]
            for i, message in enumerate(received)
        )
        pieces.append(jnp.concatenate([piece, power]).astype(jnp.float16))
    pieces = [send(piece, ALONG_Z[k]) if k else piece for k, piece in enumerate(pieces)]

    block = exchange(copies(normed, 4), "tensor", Z_GROUPS).reshape(2, 2 * tokens, width)
    blocks = [block] + [send(block, ALONG_Y[k]) for k in (1, 2, 3)]

    powers = jnp.stack([piece[tokens:] for piece in pieces]).astype(jnp.float32)
    power = jnp.min(powers, axis=0) - 2.0
    scales = jnp.exp2(power - powers)
    piece = sum(piece[:tokens].astype(jnp.float32) * scales[i, :1] for i, piece in enumerate(pieces))
    piece = send(jnp.concatenate([piece, power]).astype(jnp.float16), OWNER)
    grad_normed = piece[:tokens].astype(jnp.float32) * jnp.exp2(-piece[tokens : tokens + 1].astype(jnp.float32))

    scaled = grad_normed * ln_gain
    told = jnp.concatenate([jnp.sum(scaled, axis=1), jnp.sum(scaled * standard, axis=1)])
    told = exchange(copies(told, TENSOR), "tensor")
    sums = jnp.stack([jnp.sum(grad_normed * standard, axis=0), jnp.sum(grad_normed, axis=0)])
    others = [send(sums, ALONG_X[i][0]) for i in (1, 2, 3)]
    at = jnp.stack([(x - y + k) % 4 for k in range(4)] + [c]).astype(jnp.int32)
    grad_other = weight_part(at, blocks, query_other)
    grad_mine = weight_part(at, blocks, query, c)
    told, others, grad_other, grad_mine = lax.optimization_barrier((told, others, grad_other, grad_mine))
    grad_other = send(grad_other, CORE)
    sums = sums + others[0] + others[1] + others[2]
    sums = sums + send(sums, ALONG_X[0][1])
    told = jnp.sum(told, axis=0) / features
    grad_input = inv_std * (scaled - told[:tokens, None] - standard * told[tokens:, None])

    grad_weight = fill((1 - c).astype(jnp.int32).reshape(1), grad_other, grad_mine).reshape(4 * width, width)
    return (grad_input, grad_weight, sums[0], sums[1])


def solution(mesh):
    placed = (P("dp", "tensor"), P("tensor"), P("tensor"), P("dp", "tensor"), P("dp", "tensor"))
    return jax.shard_map(
        body,
        mesh=mesh,
        in_specs=placed,
        out_specs=(P("dp", "tensor"), P("dp", "tensor"), P("tensor"), P("tensor")),
        check_vma=False,
    )
```
